32 devices in a mesh: energy: 8 (over y, x, core), space: 4 (over z).
Axes of the slice: x: 2, y: 2, z: 4, core: 2. Of those that a mesh axis runs over, the one named last changes fastest.
Arguments:
- g_upper: bfloat16 [2, 32, 4, 384, 384], P(None, 'energy', 'space'), may hold values from -6 to 6
- p_diag: bfloat16 [2, 32, 4, 384, 384], P(None, 'energy', 'space'), may hold values from -0.8984375 to 0.8984375
- p_upper: bfloat16 [2, 32, 4, 384, 384], P(None, 'energy', 'space'), may hold values from -0.8984375 to 0.8984375
- v_diag: bfloat16 [4, 384, 384], P('space'), may hold values from -0.3125 to 0.3125
- v_upper: bfloat16 [4, 384, 384], P('space'), may hold values from -0.3125 to 0.3125
- v_pattern: int32 [4], P('space'), may hold values from 0 to 1, as said below
- element_present: int32 [4, 48], P('space'), may hold values from 0 to 1, as said below
Outputs:
- sigma_upper: bfloat16 [2, 32, 4, 384, 384], P(None, 'energy', 'space')
The draws below stay inside these ranges and needn't reach their ends.
Inputs may be any that keep to these rules, and one draw needn't show every extreme that they name: `element_present`: no block row has more than 30 present groups, and some block row has exactly 30. `v_pattern`: the first and the last block row always have their upper block; the others may lack it.
All inputs are finite; a program needn't handle non-finite values.
Results may differ from the reference program's by a relative error of at most 0.013.
Values may be sent and summed in bfloat16 or wider, within the bound.
A program may use at most 128 MiB of HBM per device.

```python
import math
import jax
import jax.numpy as jnp
from jax import lax

B = 384
RG = 8
NE = 32
NB = 4
NG = 48
LIVE = 30


def draw_v_pattern(key, part):
    inner_bits = jax.random.randint(jax.random.fold_in(key, 29), (NB,), 0, 2, dtype=jnp.int32)
    positions = jnp.arange(NB, dtype=jnp.int32)
    edges = (positions == 0) | (positions == NB - 1)
    return jnp.where(edges, jnp.ones((NB,), jnp.int32), inner_bits)


def draw_element_present(key, part):
    base = jax.random.fold_in(key, 17)
    counts = jax.random.randint(jax.random.fold_in(base, 1), (NB,), max(NG // 4, 1), LIVE + 1, dtype=jnp.int32)
    fullest = jax.random.randint(jax.random.fold_in(base, 2), (), 0, NB, dtype=jnp.int32)
    counts = jnp.where(jnp.arange(NB, dtype=jnp.int32) == fullest, LIVE, counts)

    def one_row(row_key, count):
        order = jax.random.permutation(row_key, NG).astype(jnp.int32)
        ranks = jnp.zeros((NG,), jnp.int32).at[order].set(jnp.arange(NG, dtype=jnp.int32))
        return (ranks < count).astype(jnp.int32)
    return jax.vmap(one_row)(jax.random.split(jax.random.fold_in(base, 3), NB), counts)


def steps_of(key, shape, shards, low, top_value):
    def one(dim, blocks):
        draws = jax.random.uniform(jax.random.fold_in(jax.random.fold_in(key, 6), dim), (blocks,), jnp.float32, low / len(shards), top_value / len(shards))
        return jnp.repeat(jnp.exp(draws), shape[dim] // blocks).reshape((-1,) + (1,) * (len(shape) - dim - 1))

    level = one(*shards[0])
    for cut in shards[1:]:
        level = level * one(*cut)
    return level


def scatter_about(key, dims, deviation, most, shards=(), kind=jnp.bfloat16):
    array = deviation * jax.random.normal(key, dims, jnp.float32)
    if shards:
        array = array * steps_of(key, dims, shards, -0.22, 0.18)
    return jnp.clip(array, -most, most).astype(kind)


def setup_inputs(seed: int = 0) -> dict:
    arg_keys = jax.random.split(jax.random.key(seed), 8)
    g_upper = scatter_about(arg_keys[0], (2, NE, NB, B, B), 1.0, 6.0, ((1, 8), (2, 4)))
    p_diag = scatter_about(arg_keys[1], (2, NE, NB, B, B), 0.15, 0.8984375, ((1, 8), (2, 4)))
    p_upper = scatter_about(arg_keys[2], (2, NE, NB, B, B), 0.15, 0.8984375, ((1, 8), (2, 4)))
    v_diag = scatter_about(arg_keys[3], (NB, B, B), B ** -0.5, 0.3125, ((0, 4),))
    v_upper = scatter_about(arg_keys[4], (NB, B, B), B ** -0.5, 0.3125, ((0, 4),))
    v_pattern = draw_v_pattern(jax.random.fold_in(arg_keys[7], 71), 0)
    element_present = draw_element_present(jax.random.fold_in(arg_keys[7], 71), 0)
    return dict(g_upper=g_upper, p_diag=p_diag, p_upper=p_upper, v_diag=v_diag, v_upper=v_upper, v_pattern=v_pattern, element_present=element_present)


def rounded(values):
    return lax.optimization_barrier(values.astype(jnp.bfloat16)).astype(jnp.float32)

def reference(g_upper, p_diag, p_upper, v_diag, v_upper, v_pattern, element_present):
    upper_masked = v_upper.astype(jnp.float32) * v_pattern.astype(jnp.float32)[:, None, None]
    square = v_diag.astype(jnp.float32)
    results = []
    for block_row in range(NB):
        previous = (block_row - 1) % NB
        following = (block_row + 1) % NB
        pd_own = p_diag[:, :, block_row].astype(jnp.float32)
        pu_own = p_upper[:, :, block_row].astype(jnp.float32)
        pu_prev = p_upper[:, :, previous].astype(jnp.float32)
        pd_next = p_diag[:, :, following].astype(jnp.float32)
        pu_next = p_upper[:, :, following].astype(jnp.float32)
        vu_own = upper_masked[block_row]
        vu_prev = upper_masked[previous]
        vu_next = upper_masked[following]
        vd_own = square[block_row]
        vd_next = square[following]
        vp_same = rounded(jnp.einsum('ki,cekj->ceij', vu_prev, pu_prev) + jnp.einsum('ik,cekj->ceij', vd_own, pd_own) + jnp.einsum('ik,cejk->ceij', vu_own, pu_own))
        vp_one = rounded(jnp.einsum('ik,cekj->ceij', vd_own, pu_own) + jnp.einsum('ik,cekj->ceij', vu_own, pd_next))
        vp_two = rounded(jnp.einsum('ik,cekj->ceij', vu_own, pu_next))
        screened = jnp.einsum('ceik,kj->ceij', vp_same, vu_own) + jnp.einsum('ceik,kj->ceij', vp_one, vd_next) + jnp.einsum('ceik,jk->ceij', vp_two, vu_next)
        screened = rounded(screened.at[0].add(vu_own))
        green_row = g_upper[:, :, block_row].astype(jnp.float32)
        green_cplx = green_row[0] + 1j * green_row[1]
        screen_cplx = screened[0] + 1j * screened[1]
        folded = jnp.fft.ifft(jnp.fft.fft(green_cplx, axis=0) * jnp.fft.fft(screen_cplx, axis=0), axis=0)
        sigma_row = 1j * folded / math.sqrt(NE)
        kept_rows = jnp.repeat(element_present[block_row].astype(jnp.float32), RG)
        stacked = jnp.stack([jnp.real(sigma_row), jnp.imag(sigma_row)]).astype(jnp.float32) * kept_rows[None, None, :, None]
        results.append(stacked.astype(jnp.bfloat16))
    return jnp.stack(results, axis=2)
```

```python
import math

import jax
import jax.numpy as jnp
from jax import lax
from jax.sharding import PartitionSpec as P

LIVE = 30
BF = jnp.bfloat16
F32 = jnp.float32


def shifted(value, axis, steps):
    count = lax.axis_size(axis)
    pairs = [(source, (source + steps) % count) for source in range(count)]
    return lax.ppermute(value, axis, pairs)


def product(form, left, right):
    return jnp.einsum(form, left, right, preferred_element_type=F32)


def transform_tables(energies, peers):
    local = energies // peers
    ids = jnp.arange(2 * energies, dtype=jnp.int32)
    part = ids // local % 2
    energy = ids // (2 * local) * local + ids % local
    phases = energy[:, None] * energy[None, :] % energies
    angles = 2.0 * math.pi / energies * phases.astype(F32)
    cosine = jnp.cos(angles)
    sine = jnp.sin(angles)
    out_im = part[:, None] == 1
    in_im = part[None, :] == 1
    forward = jnp.where(out_im == in_im, cosine, jnp.where(in_im, sine, -sine))
    inverse = jnp.where(out_im == in_im, -sine, jnp.where(in_im, -cosine, cosine))
    return forward.astype(BF), (inverse / (energies * math.sqrt(energies))).astype(BF)


def selection(present_row, orbitals, rows):
    width = orbitals // present_row.shape[0]
    live = jnp.repeat(present_row, width) > 0
    ids = jnp.arange(orbitals, dtype=jnp.int32)
    before = (ids[:, None] < ids[None, :]) & live[:, None]
    rank = jnp.sum(before.astype(jnp.int32), axis=0)
    return (live[None, :] & (rank[None, :] == jnp.arange(rows, dtype=jnp.int32)[:, None])).astype(BF)


def per_device(g_upper, p_diag, p_upper, v_diag, v_upper, v_pattern, element_present):
    peers = lax.axis_size("energy")
    local = p_diag.shape[1]
    orbitals = p_diag.shape[3]
    groups = element_present.shape[1]
    slots = (LIVE + peers - 1) // peers
    share = slots * (orbitals // groups)
    rows = peers * share
    batch = 2 * local
    energies = local * peers

    def flat(value):
        return value.reshape(batch, orbitals, orbitals)

    g, pd, pu = flat(g_upper), flat(p_diag), flat(p_upper)
    vd = v_diag[0]
    vu = v_upper[0] * v_pattern.astype(BF)[:, None]
    pick = selection(element_present[0], orbitals, rows)
    own_vu = product("rk,kj->rj", pick, vu).astype(BF)
    prev_vu = shifted(own_vu, "space", 1)
    present_next = shifted(element_present, "space", -1)
    vd_next = shifted(vd, "space", -1)
    own_vd = product("rk,kj->rj", pick, vd).astype(BF)
    pick_next = selection(present_next[0], orbitals, rows)
    next_vu = product("rk,jk->rj", pick_next, vu).astype(BF)
    left = product("rk,bkj->brj", next_vu, pu).astype(BF)
    left_in = shifted(left, "space", 1)
    right = product(
        "brk,kj->brj", product("rk,bkj->brj", prev_vu, pd).astype(BF), vd
    ) + product("brk,jk->brj", product("rk,bkj->brj", prev_vu, pu).astype(BF), vu)
    right_in = shifted(right.astype(BF), "space", -1)

    def spread(value):
        return lax.all_to_all(value, "energy", split_axis=0, concat_axis=0, tiled=True)

    send_green = jnp.moveaxis(
        product("rk,bkj->brj", pick, g).astype(BF).reshape(batch, peers, share, orbitals), 1, 0
    )
    green = spread(send_green)
    same = product("rk,bkj->brj", own_vd, pd) + product("rk,bjk->brj", own_vu, pu)
    one = product("rk,bkj->brj", own_vd, pu).astype(BF)
    total = product("brk,kj->brj", one, vd_next)
    real = (jnp.arange(batch, dtype=jnp.int32) < local).astype(F32)
    total = total + real[:, None, None] * own_vu.astype(F32)
    total = total + right_in.astype(F32)
    total = total + product("brk,kj->brj", (same + left_in.astype(F32)).astype(BF), vu)
    send_screen = jnp.moveaxis(total.astype(BF).reshape(batch, peers, share, orbitals), 1, 0)
    screen = spread(send_screen)

    forward, inverse = transform_tables(energies, peers)
    columns = share * orbitals

    def spectrum(values):
        freq = jnp.dot(forward, values.reshape(2 * energies, columns), preferred_element_type=F32)
        return freq.reshape(peers, 2, local, columns)

    green_freq = spectrum(green)
    screen_freq = spectrum(screen)
    g_re, g_im = green_freq[:, 0], green_freq[:, 1]
    s_re, s_im = screen_freq[:, 0], screen_freq[:, 1]
    mixed = jnp.stack([g_re * s_re - g_im * s_im, g_re * s_im + g_im * s_re], 1)
    mixed = mixed.reshape(2 * energies, columns).astype(BF)
    sigma = jnp.dot(inverse, mixed, preferred_element_type=F32).astype(BF)
    back = spread(sigma.reshape(peers, batch, share, orbitals))
    back = jnp.moveaxis(back, 0, 1).reshape(batch, rows, orbitals)
    out = product("rk,brj->bkj", pick, back).astype(BF)
    return out.reshape(2, local, 1, orbitals, orbitals)


def solution(mesh):
    in_specs = (
        P(None, "energy", "space", None, None),
        P(None, "energy", "space", None, None),
        P(None, "energy", "space", None, None),
        P("space", None, None),
        P("space", None, None),
        P("space"),
        P("space", None),
    )
    out_specs = P(None, "energy", "space", None, None)
    return jax.shard_map(
        per_device, mesh=mesh, in_specs=in_specs, out_specs=out_specs, check_vma=False
    )
```

```python
import math

import jax
import jax.numpy as jnp
import ml_dtypes
import numpy as np
from jax import lax
from jax.experimental import pallas as pl
from jax.experimental.pallas import tpu as pltpu
from jax.sharding import PartitionSpec as P

LIVE = 30
CHUNKS = 2
BF = jnp.bfloat16
F32 = jnp.float32


def shifted(value, axis, steps):
    count = lax.axis_size(axis)
    pairs = [(source, (source + steps) % count) for source in range(count)]
    return lax.ppermute(value, axis, pairs)


def product(form, left, right):
    return jnp.einsum(form, left, right, preferred_element_type=F32)


def transform_tables(energies, peers, share):
    local = energies // peers
    part_in = np.arange(2 * energies) // local % 2
    energy_in = np.arange(2 * energies) // (2 * local) * local + np.arange(2 * energies) % local
    part = np.arange(2 * energies) // energies
    energy = np.arange(2 * energies) % energies
    angles = 2.0 * math.pi / energies * (energy[:, None] * energy_in[None, :] % energies)
    cosine, sine = np.cos(angles), np.sin(angles)
    same = part[:, None] == part_in[None, :]
    forward = np.where(same, cosine, np.where(part_in[None, :] == 1, sine, -sine))
    inverse = np.where(same, -sine, np.where(part[:, None] == 1, -cosine, cosine)).T
    inverse = inverse / (energies * math.sqrt(energies))
    eye = np.eye(share)
    return (
        jnp.asarray(np.kron(forward, eye).astype(ml_dtypes.bfloat16)),
        jnp.asarray(np.kron(inverse, eye).astype(ml_dtypes.bfloat16)),
    )


def convolve_kernel(green_ref, screen_ref, forward_ref, inverse_ref, out_ref):
    half = forward_ref.shape[0] // 2
    green = jnp.dot(forward_ref[...], green_ref[...], preferred_element_type=F32)
    screen = jnp.dot(forward_ref[...], screen_ref[...], preferred_element_type=F32)
    g_re, g_im, s_re, s_im = green[:half], green[half:], screen[:half], screen[half:]
    real = (g_re * s_re - g_im * s_im).astype(BF)
    imag = (g_re * s_im + g_im * s_re).astype(BF)
    out_ref[...] = (
        jnp.dot(inverse_ref[:, :half], real, preferred_element_type=F32)
        + jnp.dot(inverse_ref[:, half:], imag, preferred_element_type=F32)
    ).astype(BF)


def convolve(green, screen, forward, inverse):
    count, columns = green.shape
    tile = 128 if columns % 128 == 0 else columns
    block = pl.BlockSpec((count, tile), lambda j: (0, j))
    table = pl.BlockSpec((count, count), lambda j: (0, 0))
    return pl.pallas_call(
        convolve_kernel,
        out_shape=jax.ShapeDtypeStruct((count, columns), BF),
        grid=(columns // tile,),
        in_specs=[block, block, table, table],
        out_specs=block,
        compiler_params=pltpu.CompilerParams(vmem_limit_bytes=48 << 20),
        cost_estimate=pl.CostEstimate(
            flops=6 * count * count * columns,
            bytes_accessed=4 * count * count + 6 * count * columns,
            transcendentals=0,
        ),
    )(green, screen, forward, inverse)


def selection(present_row, orbitals, rows):
    width = orbitals // present_row.shape[0]
    live = jnp.repeat(present_row, width) > 0
    ids = jnp.arange(orbitals, dtype=jnp.int32)
    before = (ids[:, None] < ids[None, :]) & live[:, None]
    rank = jnp.sum(before.astype(jnp.int32), axis=0)
    return (live[None, :] & (rank[None, :] == jnp.arange(rows, dtype=jnp.int32)[:, None])).astype(BF)


def per_device(g_upper, p_diag, p_upper, v_diag, v_upper, v_pattern, element_present):
    peers = lax.axis_size("energy")
    local = p_diag.shape[1]
    orbitals = p_diag.shape[3]
    width = orbitals // element_present.shape[1]
    slots = (LIVE + peers - 1) // peers
    chunks = CHUNKS if slots % CHUNKS == 0 else 1
    share = slots // chunks * width
    rows = peers * share
    batch = 2 * local
    energies = local * peers

    def flat(value):
        return value.reshape(batch, orbitals, orbitals)

    def spread(value):
        return lax.all_to_all(value, "energy", split_axis=0, concat_axis=0, tiled=True)

    def by_peer(value):
        return jnp.moveaxis(value.reshape(batch, peers, share, orbitals), 1, 0)

    g, pd, pu = flat(g_upper), flat(p_diag), flat(p_upper)
    vd = v_diag[0]
    vu = v_upper[0] * v_pattern.astype(BF)[:, None]
    pick = selection(element_present[0], orbitals, chunks * rows)
    own_vu = product("rk,kj->rj", pick, vu).astype(BF)
    prev_vu = shifted(own_vu[: LIVE * width], "space", 1)
    present_next = shifted(element_present, "space", -1)
    pick_next = selection(present_next[0], orbitals, LIVE * width)
    next_vu = product("rk,jk->rj", pick_next, vu).astype(BF)

    left_in, right_in, sent = [], [], []
    feed, prev_feed = next_vu, prev_vu
    for c in range(chunks):
        part = slice(c * rows, min((c + 1) * rows, LIVE * width))
        left = product("rk,bkj->brj", feed[part], pu).astype(BF)
        right = product(
            "brk,kj->brj", product("rk,bkj->brj", prev_feed[part], pd).astype(BF), vd
        ) + product("brk,jk->brj", product("rk,bkj->brj", prev_feed[part], pu).astype(BF), vu)
        right = right.astype(BF)
        left, right, feed, prev_feed, vd_last = lax.optimization_barrier(
            (left, right, feed, prev_feed, vd)
        )
        left_in.append(shifted(left, "space", 1))
        right_in.append(shifted(right, "space", -1))
        sent += [left, right]

    piece = orbitals // peers
    vd_share = lax.dynamic_slice_in_dim(vd_last, lax.axis_index("energy") * piece, piece, 0)
    vd_next = lax.all_gather(shifted(vd_share, "space", -1), "energy", axis=0, tiled=True)

    own_vd = product("rk,kj->rj", pick, vd).astype(BF)
    forward, inverse = transform_tables(energies, peers, share)
    real = (jnp.arange(batch, dtype=jnp.int32) < local).astype(F32)

    def padded(value):
        return jnp.pad(value, ((0, 0), (0, rows - value.shape[1]), (0, 0)))

    greens = [
        spread(by_peer(product("rk,bkj->brj", pick[c * rows : (c + 1) * rows], g).astype(BF)))
        for c in range(chunks)
    ]
    left_in[0], right_in[0], *sent = lax.optimization_barrier((left_in[0], right_in[0], *sent))
    sigmas, screens = [], []
    for c in range(chunks):
        part = slice(c * rows, (c + 1) * rows)
        same = product("rk,bkj->brj", own_vd[part], pd) + product(
            "rk,bjk->brj", own_vu[part], pu
        )
        one = product("rk,bkj->brj", own_vd[part], pu).astype(BF)
        total = product("brk,kj->brj", one, vd_next)
        total = total + real[:, None, None] * own_vu[part].astype(F32)
        total = total + padded(right_in[c]).astype(F32)
        total = total + product(
            "brk,kj->brj", (same + padded(left_in[c]).astype(F32)).astype(BF), vu
        )
        send_screen = by_peer(total.astype(BF))
        if c == 0:
            send_screen, *greens = lax.optimization_barrier((send_screen, *greens))
        shape = (peers * batch * share, orbitals)
        screen = spread(send_screen)
        if c + 1 < chunks:
            screen, left_in[c + 1], right_in[c + 1] = lax.optimization_barrier(
                (screen, left_in[c + 1], right_in[c + 1])
            )
        screens.append(screen)
        sigma = None
        if c + 1 < chunks:
            sigma = convolve(greens[c].reshape(shape), screen.reshape(shape), forward, inverse)
        sigmas.append(sigma)
    for c in range(chunks - 1):
        sigmas[c], screens[-1] = lax.optimization_barrier((sigmas[c], screens[-1]))
    sigmas[-1] = convolve(greens[-1].reshape(shape), screens[-1].reshape(shape), forward, inverse)
    backs = [spread(sigma.reshape(peers, batch, share, orbitals)) for sigma in sigmas]
    backs = [jnp.moveaxis(back, 0, 1).reshape(batch, rows, orbitals) for back in backs]
    out = None
    for c in range(chunks):
        term = product("rk,brj->bkj", pick[c * rows : (c + 1) * rows], backs[c])
        out = term if out is None else out + term
    return out.astype(BF).reshape(2, local, 1, orbitals, orbitals)


def solution(mesh):
    in_specs = (
        P(None, "energy", "space", None, None),
        P(None, "energy", "space", None, None),
        P(None, "energy", "space", None, None),
        P("space", None, None),
        P("space", None, None),
        P("space"),
        P("space", None),
    )
    out_specs = P(None, "energy", "space", None, None)
    return jax.shard_map(
        per_device, mesh=mesh, in_specs=in_specs, out_specs=out_specs, check_vma=False
    )
```

```python
import math

import jax
import jax.numpy as jnp
import ml_dtypes
import numpy as np
from jax import lax
from jax.experimental import pallas as pl
from jax.experimental.pallas import tpu as pltpu
from jax.sharding import PartitionSpec as P

LIVE = 30
CHUNKS = 2
BF = jnp.bfloat16
F32 = jnp.float32


def shifted(value, axis, steps):
    count = lax.axis_size(axis)
    pairs = [(source, (source + steps) % count) for source in range(count)]
    return lax.ppermute(value, axis, pairs)


def product(form, left, right):
    return jnp.einsum(form, left, right, preferred_element_type=F32)


def transform_tables(energies, peers, share):
    local = energies // peers
    part_in = np.arange(2 * energies) // local % 2
    energy_in = np.arange(2 * energies) // (2 * local) * local + np.arange(2 * energies) % local
    part = np.arange(2 * energies) // energies
    energy = np.arange(2 * energies) % energies
    angles = 2.0 * math.pi / energies * (energy[:, None] * energy_in[None, :] % energies)
    cosine, sine = np.cos(angles), np.sin(angles)
    same = part[:, None] == part_in[None, :]
    forward = np.where(same, cosine, np.where(part_in[None, :] == 1, sine, -sine))
    inverse = np.where(same, -sine, np.where(part[:, None] == 1, -cosine, cosine)).T
    inverse = inverse / (energies * math.sqrt(energies))
    eye = np.eye(share)
    return (
        jnp.asarray(np.kron(forward, eye).astype(ml_dtypes.bfloat16)),
        jnp.asarray(np.kron(inverse, eye).astype(ml_dtypes.bfloat16)),
    )


def convolve_kernel(green_ref, screen_ref, forward_ref, inverse_ref, out_ref):
    half = forward_ref.shape[0] // 2
    green = jnp.dot(forward_ref[...], green_ref[...], preferred_element_type=F32)
    screen = jnp.dot(forward_ref[...], screen_ref[...], preferred_element_type=F32)
    g_re, g_im, s_re, s_im = green[:half], green[half:], screen[:half], screen[half:]
    real = (g_re * s_re - g_im * s_im).astype(BF)
    imag = (g_re * s_im + g_im * s_re).astype(BF)
    out_ref[...] = (
        jnp.dot(inverse_ref[:, :half], real, preferred_element_type=F32)
        + jnp.dot(inverse_ref[:, half:], imag, preferred_element_type=F32)
    ).astype(BF)


def convolve(green, screen, forward, inverse):
    count, columns = green.shape
    tile = columns
    block = pl.BlockSpec((count, tile), lambda j: (0, j))
    table = pl.BlockSpec((count, count), lambda j: (0, 0))
    return pl.pallas_call(
        convolve_kernel,
        out_shape=jax.ShapeDtypeStruct((count, columns), BF),
        grid=(columns // tile,),
        in_specs=[block, block, table, table],
        out_specs=block,
        compiler_params=pltpu.CompilerParams(vmem_limit_bytes=48 << 20),
        cost_estimate=pl.CostEstimate(
            flops=6 * count * count * columns,
            bytes_accessed=4 * count * count + 6 * count * columns,
            transcendentals=0,
        ),
    )(green, screen, forward, inverse)


def selection(present_row, orbitals, rows):
    width = orbitals // present_row.shape[0]
    live = jnp.repeat(present_row, width) > 0
    ids = jnp.arange(orbitals, dtype=jnp.int32)
    before = (ids[:, None] < ids[None, :]) & live[:, None]
    rank = jnp.sum(before.astype(jnp.int32), axis=0)
    return (live[None, :] & (rank[None, :] == jnp.arange(rows, dtype=jnp.int32)[:, None])).astype(BF)


def per_device(g_upper, p_diag, p_upper, v_diag, v_upper, v_pattern, element_present):
    peers = lax.axis_size("energy")
    local = p_diag.shape[1]
    orbitals = p_diag.shape[3]
    width = orbitals // element_present.shape[1]
    slots = (LIVE + peers - 1) // peers
    chunks = CHUNKS if slots % CHUNKS == 0 else 1
    share = slots // chunks * width
    rows = peers * share
    batch = 2 * local
    energies = local * peers

    def flat(value):
        return value.reshape(batch, orbitals, orbitals)

    def spread(value):
        return lax.all_to_all(value, "energy", split_axis=0, concat_axis=0, tiled=True)

    def by_peer(value):
        return jnp.moveaxis(value.reshape(batch, peers, share, orbitals), 1, 0)

    g, pd, pu = flat(g_upper), flat(p_diag), flat(p_upper)
    vd = v_diag[0]
    vu = v_upper[0] * v_pattern.astype(BF)[:, None]
    pick = selection(element_present[0], orbitals, chunks * rows)
    own_vu = product("rk,kj->rj", pick, vu).astype(BF)
    prev_vu = shifted(own_vu[: LIVE * width], "space", 1)
    present_next = shifted(element_present, "space", -1)
    vd_next, present_next = lax.optimization_barrier((shifted(vd, "space", -1), present_next))
    pick_next = selection(present_next[0], orbitals, LIVE * width)
    next_vu = product("rk,jk->rj", pick_next, vu).astype(BF)

    left_in, right_in, sent = [], [], []
    feed, prev_feed = next_vu, prev_vu
    for c in range(chunks):
        part = slice(c * rows, min((c + 1) * rows, LIVE * width))
        left = product("rk,bkj->brj", feed[part], pu).astype(BF)
        right = product(
            "brk,kj->brj", product("rk,bkj->brj", prev_feed[part], pd).astype(BF), vd
        ) + product("brk,jk->brj", product("rk,bkj->brj", prev_feed[part], pu).astype(BF), vu)
        right = right.astype(BF)
        left, right, feed, prev_feed, pick, vd_late = lax.optimization_barrier(
            (left, right, feed, prev_feed, pick, vd)
        )
        left_in.append(shifted(left, "space", 1))
        right_in.append(shifted(right, "space", -1))
        sent += [left, right]

    own_vd = product("rk,kj->rj", pick, vd_late).astype(BF)
    forward, inverse = transform_tables(energies, peers, share)
    real = (jnp.arange(batch, dtype=jnp.int32) < local).astype(F32)

    def padded(value):
        return jnp.pad(value, ((0, 0), (0, rows - value.shape[1]), (0, 0)))

    greens = [
        spread(by_peer(product("rk,bkj->brj", pick[c * rows : (c + 1) * rows], g).astype(BF)))
        for c in range(chunks)
    ]
    left_in[0], right_in[0], *sent = lax.optimization_barrier((left_in[0], right_in[0], *sent))
    sigmas, screens = [], []
    for c in range(chunks):
        part = slice(c * rows, (c + 1) * rows)
        same = product("rk,bkj->brj", own_vd[part], pd) + product(
            "rk,bjk->brj", own_vu[part], pu
        )
        one = product("rk,bkj->brj", own_vd[part], pu).astype(BF)
        total = product("brk,kj->brj", one, vd_next)
        total = total + real[:, None, None] * own_vu[part].astype(F32)
        total = total + padded(right_in[c]).astype(F32)
        total = total + product(
            "brk,kj->brj", (same + padded(left_in[c]).astype(F32)).astype(BF), vu
        )
        send_screen = by_peer(total.astype(BF))
        if c == 0:
            send_screen, *greens = lax.optimization_barrier((send_screen, *greens))
        shape = (peers * batch * share, orbitals)
        screen = spread(send_screen)
        if c + 1 < chunks:
            screen, left_in[c + 1], right_in[c + 1] = lax.optimization_barrier(
                (screen, left_in[c + 1], right_in[c + 1])
            )
        screens.append(screen)
        sigma = None
        if c + 1 < chunks:
            sigma = convolve(greens[c].reshape(shape), screen.reshape(shape), forward, inverse)
        sigmas.append(sigma)
    for c in range(chunks - 1):
        sigmas[c], screens[-1] = lax.optimization_barrier((sigmas[c], screens[-1]))
    sigmas[-1] = convolve(greens[-1].reshape(shape), screens[-1].reshape(shape), forward, inverse)
    backs = [spread(sigma.reshape(peers, batch, share, orbitals)) for sigma in sigmas]
    backs = [jnp.moveaxis(back, 0, 1).reshape(batch, rows, orbitals) for back in backs]
    out = None
    for c in range(chunks):
        term = product("rk,brj->bkj", pick[c * rows : (c + 1) * rows], backs[c])
        out = term if out is None else out + term
    return out.astype(BF).reshape(2, local, 1, orbitals, orbitals)


def solution(mesh):
    in_specs = (
        P(None, "energy", "space", None, None),
        P(None, "energy", "space", None, None),
        P(None, "energy", "space", None, None),
        P("space", None, None),
        P("space", None, None),
        P("space"),
        P("space", None),
    )
    out_specs = P(None, "energy", "space", None, None)
    return jax.shard_map(
        per_device, mesh=mesh, in_specs=in_specs, out_specs=out_specs, check_vma=False
    )
```
